32 devices in a mesh: rep: 4 (over y, x), fsdp: 8 (over z, core).
Axes of the slice: x: 2, y: 2, z: 4, core: 2. Of those that a mesh axis runs over, the one named last changes fastest.
Arguments:
- inputs: bfloat16 [4, 4096, 5120], P('rep', 'fsdp'), may hold values from -6 to 6
- target: bfloat16 [4, 4096, 1024], P('rep', 'fsdp'), may hold values from -12 to 12
- norm_gain: float32 [5120], replicated, may hold values from 0.5 to 1.5
- numerators: float32 [4, 5120, 1024], P('rep', 'fsdp'), may hold values from -0.18 to 0.18
- moment: float32 [4, 5120, 1024], P('rep', 'fsdp'), may hold values from -600 to 600
- second: float32 [4, 5120, 1024], P('rep', 'fsdp'), may hold values from 1000 to 100000
- push_weight: float32 [4], P('rep'), may hold values from 0.5 to 2
- step_index: int32 [1], replicated, may hold values from 1 to 999
Outputs:
- new_numerators: float32 [4, 5120, 1024], P('rep', 'fsdp')
- new_moment: float32 [4, 5120, 1024], P('rep', 'fsdp')
- new_second: float32 [4, 5120, 1024], P('rep', 'fsdp')
- new_weight: float32 [4], P('rep')
The draws below stay inside these ranges and needn't reach their ends.
All inputs are finite; a program needn't handle non-finite values.
Results may differ from the reference program's by a relative error of at most 0.0003.
Values may be sent and summed in bfloat16 or wider, within the bound.
A program may use at most 128 MiB of HBM per device.

```python
import math
import jax
import jax.numpy as jnp
from jax import lax

D = 5120
KV = 1024
TOKENS = 4096
N_REP = 4


def steps_of(rng, dims, shards, low, top_value):
    gain, own = 1.0, jax.random.fold_in(rng, 6)
    for dim, shards_of in shards:
        steps = jnp.exp(jax.random.uniform(jax.random.fold_in(own, dim), (shards_of,), jnp.float32, low / len(shards), top_value / len(shards)))
        gain = gain * jnp.repeat(steps, dims[dim] // shards_of).reshape([-1 if axis == dim else 1 for axis in range(len(dims))])
    return gain


def scatter_about(key, extent, scale, bound, pieces=(), kind=jnp.bfloat16):
    level = steps_of(key, extent, pieces, -0.22, 0.18) if pieces else 1.0
    drawn = jax.random.normal(key, extent, jnp.float32) * scale * level
    return jnp.minimum(jnp.maximum(drawn, -bound), bound).astype(kind)


def setup_inputs(seed: int = 0) -> dict:
    key_list = jax.random.split(jax.random.key(seed), 9)
    return {
        "inputs": scatter_about(key_list[0], (N_REP, TOKENS, D), 1.0, 6.0, ((0, 4), (1, 8))),
        "target": scatter_about(key_list[1], (N_REP, TOKENS, KV), 2.0, 12.0, ((0, 4), (1, 8))),
        "norm_gain": jnp.clip(1.0 + 0.1 * jax.random.normal(key_list[2], (D,), jnp.float32), 0.5, 1.5),
        "numerators": scatter_about(key_list[3], (N_REP, D, KV), 0.03, 0.18, ((0, 4), (1, 8)), jnp.float32),
        "moment": scatter_about(key_list[4], (N_REP, D, KV), 100.0, 600.0, ((0, 4), (1, 8)), jnp.float32),
        "second": jnp.clip(jnp.exp(math.log(100000.0) - 4.6051702 * jax.random.uniform(key_list[5], (N_REP, D, KV), jnp.float32) ** steps_of(key_list[5], (N_REP, D, KV), ((0, 4), (1, 8)), -0.2, 0.2)), 1000.0, 100000.0),
        "push_weight": jnp.clip(jnp.exp(math.log(2.0) - 1.3862944 * jax.random.uniform(key_list[6], (N_REP,), jnp.float32) ** steps_of(key_list[6], (N_REP,), ((0, 4),), -0.2, 0.2)), 0.5, 2.0),
        "step_index": jax.random.randint(key_list[7], (1,), 1, 1000).astype(jnp.int32),
    }


eps_norm = 1e-06
beta_one = 0.9
beta_two = 0.95
learn_rate = 0.001
decay_rate = 0.1
eps_adam = 1e-08

def reference(inputs, target, norm_gain, numerators, moment, second, push_weight, step_index):

    def group_grad(packed):
        group_in, group_target, group_numer, group_weight = packed
        values = group_in.astype(jnp.float32)
        inv_rms = lax.rsqrt(lax.optimization_barrier(jnp.mean(values * values, axis=-1, keepdims=True)) + eps_norm)
        normed = (values * inv_rms * norm_gain).astype(jnp.bfloat16)
        weight_low = (group_numer / group_weight).astype(jnp.bfloat16)
        projected = jnp.dot(normed, weight_low, preferred_element_type=jnp.float32)
        key_error = (projected - group_target.astype(jnp.float32)).astype(jnp.bfloat16)
        return jnp.dot(normed.T, key_error, preferred_element_type=jnp.float32)
    gradient = lax.map(group_grad, (inputs, target, numerators, push_weight))
    new_moment = beta_one * moment + (1.0 - beta_one) * gradient
    new_second = beta_two * second + (1.0 - beta_two) * gradient * gradient
    steps_done = step_index[0].astype(jnp.float32)
    fix_one = 1.0 - jnp.power(jnp.float32(beta_one), steps_done)
    fix_two = 1.0 - jnp.power(jnp.float32(beta_two), steps_done)
    group_weight = push_weight[:, None, None]
    current = numerators / group_weight
    direction = new_moment / fix_one / (jnp.sqrt(new_second / fix_two) + eps_adam)
    updated = current - learn_rate * (direction + decay_rate * current)
    shares = group_weight * updated
    bit_count = N_REP.bit_length() - 1
    bit_index = step_index[0] % bit_count
    partner = jnp.bitwise_xor(jnp.arange(N_REP, dtype=jnp.int32), jnp.left_shift(jnp.int32(1), bit_index).astype(jnp.int32))
    new_numerators = (shares + shares[partner]) * 0.5
    new_weight = (push_weight + push_weight[partner]) * 0.5
    return (new_numerators, new_moment, new_second, new_weight)
```

```python
from functools import partial

import jax
import jax.numpy as jnp
from jax import lax
from jax.experimental import pallas as pl
from jax.experimental.pallas import tpu as pltpu
from jax.sharding import PartitionSpec as P

eps_norm = 1e-06
beta_one = 0.9
beta_two = 0.95
learn_rate = 0.001
decay_rate = 0.1
eps_adam = 1e-08
lanes = 128
MESH = pl.DeviceIdType.MESH


def tile_of(size, top):
    best = 16
    for rows in range(16, top + 1, 16):
        if size % rows == 0:
            best = rows
    return best


def kernel(
    chips, levels, scal, bit_ref, gain_ref, x_hbm, t_hbm, n_hbm, m_hbm, s_hbm,
    on_hbm, om_hbm, os_hbm, ow_ref,
    normed, wst, wall, tgt, err, part, recv, fin, numer, mom, sec, other, wx,
    load_sem, local_sem, out_sem, wsib_s, wsib_r, tsib, nsib_s, nsib_r,
    wsend, wrecv, gsend, grecv, fsend, frecv, xsend, xrecv, psend, precv,
):
    tokens, depth = x_hbm.shape
    rows, cols = n_hbm.shape
    half = cols // 2
    chunks = half // lanes
    chip_rows = 2 * rows
    me_r = lax.axis_index("rep")
    me_f = lax.axis_index("fsdp")
    c = me_f // 2
    k = me_f % 2
    sibling = (me_r, 2 * c + 1 - k)
    left = (me_r, jnp.maximum(me_f - 2, 0))
    right = (me_r, jnp.minimum(me_f + 2, 2 * chips - 1))
    partners = []
    for level in range(levels):
        step = 1 << level
        partners.append((me_r + step * (1 - 2 * ((me_r // step) % 2)), me_f))
    has_left = c > 0
    has_right = c < chips - 1
    own_tokens = pl.ds(pl.multiple_of(k * tokens, tokens), tokens)

    load_n = pltpu.make_async_copy(n_hbm, numer, load_sem.at[0])
    load_x = pltpu.make_async_copy(x_hbm, normed.at[own_tokens], load_sem.at[1])
    load_m = pltpu.make_async_copy(m_hbm, mom, load_sem.at[2])
    load_s = pltpu.make_async_copy(s_hbm, sec, load_sem.at[3])
    own_cols = pl.ds(pl.multiple_of(k * half, half), half)
    load_t = pltpu.make_async_copy(t_hbm.at[:, own_cols], tgt.at[own_tokens], load_sem.at[4])
    load_n.start()
    load_x.start()

    barrier = pltpu.get_barrier_semaphore()

    def greet(who):
        pl.semaphore_signal(barrier, inc=1, device_id=who, device_id_type=MESH)

    greet(sibling)
    for who in partners:
        greet(who)
    pl.when(has_left)(lambda: greet(left))
    pl.when(has_right)(lambda: greet(right))

    own_weight = scal[0]
    load_n.wait()
    small = tile_of(rows, 32)

    @pl.loop(0, rows // small)
    def _(i):
        at = pl.ds(pl.multiple_of(i * small, small), small)
        wst[at, :] = (numer[at, :] / own_weight).astype(jnp.bfloat16)

    peers = 1 + levels + jnp.minimum(c, 1) + jnp.minimum(chips - 1 - c, 1)
    pl.semaphore_wait(barrier, peers)

    def remote(src, dst, send, recv_sem, who):
        return pltpu.make_async_remote_copy(
            src_ref=src, dst_ref=dst, send_sem=send, recv_sem=recv_sem,
            device_id=who, device_id_type=MESH,
        )

    my_rows = pl.ds(pl.multiple_of(c * chip_rows + k * rows, rows), rows)

    def part_cols(which, j):
        return pl.ds(pl.multiple_of(which * half + j * lanes, lanes), lanes)

    def w_sibling(j):
        return remote(
            wst.at[:, part_cols(1 - k, j)], wall.at[j, my_rows], wsib_s.at[j], wsib_r.at[j], sibling
        )

    def w_own(j):
        return pltpu.make_async_copy(
            wst.at[:, part_cols(k, j)], wall.at[j, my_rows], local_sem.at[j]
        )

    for j in range(chunks):
        w_sibling(j).start()
        w_own(j).start()

    other_cols = pl.ds(pl.multiple_of((1 - k) * half, half), half)
    send_t = remote(t_hbm.at[:, other_cols], tgt.at[own_tokens], tsib.at[0], tsib.at[1], sibling)

    def block(b):
        return pl.ds(pl.multiple_of(b * chip_rows, chip_rows), chip_rows)

    def w_right(j, b):
        return remote(
            wall.at[j, block(b)], wall.at[j, block(b)], wsend.at[0, j, b], wrecv.at[j, b], right
        )

    def w_left(j, b):
        return remote(
            wall.at[j, block(b)], wall.at[j, block(b)], wsend.at[1, j, b], wrecv.at[j, b], left
        )

    def w_step(j, s):
        if s == 0:
            w_sibling(j).wait_recv()
            w_own(j).wait()
            pl.when(has_right)(lambda: w_right(j, c).start())
            pl.when(has_left)(lambda: w_left(j, c).start())
            return

        @pl.when(c - s >= 0)
        def _():
            b = jnp.maximum(c - s, 0)
            w_right(j, b).wait_recv()
            pl.when(has_right)(lambda: w_right(j, b).start())

        @pl.when(c + s <= chips - 1)
        def _():
            b = jnp.minimum(c + s, chips - 1)
            w_left(j, b).wait_recv()
            pl.when(has_left)(lambda: w_left(j, b).start())

    def w_finish(j):
        w_sibling(j).wait_send()
        for b in range(chips):
            pl.when(has_right & (b <= c))(lambda: w_right(j, b).wait_send())
            pl.when(has_left & (b >= c))(lambda: w_left(j, b).wait_send())

    w_step(0, 0)

    load_x.wait()
    pieces = 4
    piece = tokens // pieces
    group = tile_of(piece, 16)

    def n_piece(q):
        at = pl.ds(pl.multiple_of(k * tokens + q * piece, piece), piece)
        return remote(normed.at[at], normed.at[at], nsib_s.at[q], nsib_r.at[q], sibling)

    for q in range(pieces):

        @pl.loop(0, piece // group)
        def _(i):
            start = pl.multiple_of(k * tokens + q * piece + i * group, group)
            at = pl.ds(start, group)
            values = normed[at, :].astype(jnp.float32)
            mean = jnp.mean(values * values, axis=-1, keepdims=True)
            inv_rms = lax.rsqrt(mean + eps_norm)
            normed[at, :] = (values * inv_rms * gain_ref[...]).astype(jnp.bfloat16)

        n_piece(q).start()

    load_t.start()
    send_t.start()
    load_m.start()
    load_s.start()
    wx[0] = jnp.full(wx.shape[1:], own_weight, jnp.float32)

    def p_copy(level):
        return remote(
            wx.at[0], wx.at[1 + level], psend.at[level], precv.at[level], partners[level]
        )

    for level in range(levels):
        p_copy(level).start()

    for s in range(1, chips):
        w_step(0, s)
    for q in range(pieces):
        n_piece(q).wait()
    load_t.wait()
    send_t.wait()

    ptile = tile_of(2 * tokens, 256)
    gtile = 512 if depth % 512 == 0 else lanes

    def compute(j):
        @pl.loop(0, 2 * tokens // ptile)
        def _(i):
            at = pl.ds(pl.multiple_of(i * ptile, ptile), ptile)
            projected = jnp.dot(normed[at, :], wall[j], preferred_element_type=jnp.float32)
            wanted = tgt[at, j * lanes : (j + 1) * lanes].astype(jnp.float32)
            err[at, :] = (projected - wanted).astype(jnp.bfloat16)

        @pl.loop(0, depth // gtile)
        def _(i):
            at = pl.ds(pl.multiple_of(i * gtile, gtile), gtile)
            part[j, at, :] = lax.dot_general(
                normed[:, at], err[...], (((0,), (0,)), ((), ())),
                preferred_element_type=jnp.float32,
            )

    def g_right(j, d):
        return remote(
            part.at[j, block(d)], recv.at[j, block(d + 1)], gsend.at[j, 0, d], grecv.at[j, 0, d], right
        )

    def g_left(j, d):
        return remote(
            part.at[j, block(d)], recv.at[j, block(d)], gsend.at[j, 1, d], grecv.at[j, 1, d], left
        )

    add_rows = tile_of(chip_rows, 160)

    def add_in(j, d, b):
        @pl.loop(0, chip_rows // add_rows)
        def _(i):
            to = pl.ds(pl.multiple_of(d * chip_rows + i * add_rows, add_rows), add_rows)
            src = pl.ds(pl.multiple_of(b * chip_rows + i * add_rows, add_rows), add_rows)
            part[j, to, :] = part[j, to, :] + recv[j, src, :]

    def g_first(j):
        for d in range(chips - 1, 0, -1):
            pl.when(c == 0)(lambda: g_right(j, d).start())
        for d in range(chips - 1):
            pl.when(c == chips - 1)(lambda: g_left(j, d).start())

    def g_step(j, s):
        d = chips - 1 - s

        @pl.when((c > 0) & (c < d))
        def _():
            g_right(j, d).wait_recv()
            add_in(j, d, d + 1)
            g_right(j, d).start()

        @pl.when((c < chips - 1) & (c > s))
        def _():
            g_left(j, s).wait_recv()
            add_in(j, s, s)
            g_left(j, s).start()

    def f_copy(j):
        at = pl.ds(pl.multiple_of(c * chip_rows + (1 - k) * rows, rows), rows)
        return remote(part.at[j, at], fin.at[k, j], fsend.at[j], frecv.at[j], sibling)

    def f_arrived(j):
        at = pl.ds(pl.multiple_of(c * chip_rows + (1 - k) * rows, rows), rows)
        return remote(part.at[j, at], fin.at[1 - k, j], fsend.at[j], frecv.at[j], sibling)

    def f_own(j):
        return pltpu.make_async_copy(part.at[j, my_rows], fin.at[k, j], local_sem.at[j])

    def g_final(j):
        @pl.when(has_left)
        def _():
            g_right(j, c).wait_recv()
            add_in(j, c, c + 1)

        @pl.when(has_right)
        def _():
            g_left(j, c).wait_recv()
            add_in(j, c, c)

        f_copy(j).start()
        f_own(j).start()

    def g_finish(j):
        f_copy(j).wait_send()
        for d in range(chips):
            pl.when(has_right & (d > c))(lambda: g_right(j, d).wait_send())
            pl.when(has_left & (d < c))(lambda: g_left(j, d).wait_send())

    def at_cols(h, j):
        return pl.ds(h * half + j * lanes, lanes)

    def out_m(h, j):
        cs = at_cols(h, j)
        return pltpu.make_async_copy(mom.at[:, cs], om_hbm.at[:, cs], out_sem.at[0, h, j])

    def out_s(h, j):
        cs = at_cols(h, j)
        return pltpu.make_async_copy(sec.at[:, cs], os_hbm.at[:, cs], out_sem.at[1, h, j])

    def out_n(h, j):
        cs = at_cols(h, j)
        return pltpu.make_async_copy(fin.at[h, j], on_hbm.at[:, cs], out_sem.at[2, h, j])

    def x_copy(h, j, level):
        cs = at_cols(h, j)
        return remote(
            numer.at[:, cs], other.at[level, :, cs],
            xsend.at[level, h, j], xrecv.at[level, h, j], partners[level],
        )

    adam_rows = tile_of(rows, 80)
    fix_one = scal[1]
    fix_two = scal[2]

    def adam(j):
        f_own(j).wait()
        f_arrived(j).wait_recv()
        for h in range(2):
            cs = at_cols(h, j)

            @pl.loop(0, rows // adam_rows)
            def _(i):
                at = pl.ds(pl.multiple_of(i * adam_rows, adam_rows), adam_rows)
                gradient = fin[h, j, at, :]
                new_moment = beta_one * mom[at, cs] + (1.0 - beta_one) * gradient
                new_second = beta_two * sec[at, cs] + (1.0 - beta_two) * gradient * gradient
                mom[at, cs] = new_moment
                sec[at, cs] = new_second
                current = numer[at, cs] / own_weight
                direction = new_moment / fix_one / (jnp.sqrt(new_second / fix_two) + eps_adam)
                updated = current - learn_rate * (direction + decay_rate * current)
                numer[at, cs] = own_weight * updated

            for level in range(levels):
                x_copy(h, j, level).start()
            out_m(h, j).start()
            out_s(h, j).start()

    def mix(j):
        for h in range(2):
            cs = at_cols(h, j)
            for level in range(levels):
                x_copy(h, j, level).wait_recv()

            @pl.loop(0, rows // adam_rows)
            def _(i):
                at = pl.ds(pl.multiple_of(i * adam_rows, adam_rows), adam_rows)
                theirs = other[0, at, cs]
                for level in range(1, levels):
                    theirs = jnp.where(bit_ref[0] == level, other[level, at, cs], theirs)
                fin[h, j, at, :] = (numer[at, cs] + theirs) * 0.5

            out_n(h, j).start()

    compute(0)
    g_first(0)
    load_m.wait()
    load_s.wait()
    if chunks > 1:
        for s in range(chips):
            w_step(1, s)
    for j in range(chunks):
        if j + 1 < chunks:
            compute(j + 1)
            g_first(j + 1)
        for s in range(chips):
            if j + 2 < chunks:
                w_step(j + 2, s)
            if s < chips - 1:
                g_step(j, s)
        g_final(j)
        adam(j)
        if j > 0:
            mix(j - 1)
    for level in range(levels):
        p_copy(level).wait()
    theirs = wx[1]
    for level in range(1, levels):
        theirs = jnp.where(bit_ref[0] == level, wx[1 + level], theirs)
    ow_ref[...] = (wx[0] + theirs) * 0.5
    for j in range(chunks):
        w_finish(j)
        g_finish(j)
    mix(chunks - 1)
    for j in range(chunks):
        for h in range(2):
            for level in range(levels):
                x_copy(h, j, level).wait_send()
            out_m(h, j).wait()
            out_s(h, j).wait()
            out_n(h, j).wait()


def local(inputs, target, norm_gain, numerators, moment, second, push_weight, step_index):
    chips = lax.axis_size("fsdp") // 2
    levels = lax.axis_size("rep").bit_length() - 1
    _, tokens, depth = inputs.shape
    _, rows, cols = numerators.shape
    half = cols // 2
    chunks = half // lanes
    steps_done = step_index[0].astype(jnp.float32)
    fix_one = 1.0 - jnp.power(jnp.float32(beta_one), steps_done)
    fix_two = 1.0 - jnp.power(jnp.float32(beta_two), steps_done)
    scal = jnp.stack([push_weight[0], fix_one, fix_two])
    bit = (step_index % levels).astype(jnp.int32)
    shard = jax.ShapeDtypeStruct((rows, cols), jnp.float32)
    dma = pltpu.SemaphoreType.DMA
    smem = pl.BlockSpec(memory_space=pltpu.SMEM)
    vmem = pl.BlockSpec(memory_space=pltpu.VMEM)
    hbm = pl.BlockSpec(memory_space=pltpu.HBM)
    bf16, f32 = jnp.bfloat16, jnp.float32
    flops = 2 * 2 * 2 * tokens * depth * half
    outs = pl.pallas_call(
        partial(kernel, chips, levels),
        out_shape=(shard, shard, shard, jax.ShapeDtypeStruct((8, lanes), f32)),
        in_specs=[smem, smem, vmem, hbm, hbm, hbm, hbm, hbm],
        out_specs=(hbm, hbm, hbm, vmem),
        scratch_shapes=[
            pltpu.VMEM((2 * tokens, depth), bf16),
            pltpu.VMEM((rows, cols), bf16),
            pltpu.VMEM((chunks, depth, lanes), bf16),
            pltpu.VMEM((2 * tokens, half), bf16),
            pltpu.VMEM((2 * tokens, lanes), bf16),
            pltpu.VMEM((chunks, depth, lanes), f32),
            pltpu.VMEM((chunks, depth + 2 * rows, lanes), f32),
            pltpu.VMEM((2, chunks, rows, lanes), f32),
            pltpu.VMEM((rows, cols), f32),
            pltpu.VMEM((rows, cols), f32),
            pltpu.VMEM((rows, cols), f32),
            pltpu.VMEM((levels, rows, cols), f32),
            pltpu.VMEM((1 + levels, 8, lanes), f32),
            dma((5,)),
            dma((chunks,)),
            dma((3, 2, chunks)),
            dma((chunks,)),
            dma((chunks,)),
            dma((2,)),
            dma((4,)),
            dma((4,)),
            dma((2, chunks, chips)),
            dma((chunks, chips)),
            dma((chunks, 2, chips)),
            dma((chunks, 2, chips)),
            dma((chunks,)),
            dma((chunks,)),
            dma((levels, 2, chunks)),
            dma((levels, 2, chunks)),
            dma((levels,)),
            dma((levels,)),
        ],
        compiler_params=pltpu.CompilerParams(
            collective_id=0, has_side_effects=True, vmem_limit_bytes=62 * 1024 * 1024
        ),
        cost_estimate=pl.CostEstimate(
            flops=flops, bytes_accessed=2 * tokens * depth + 28 * rows * cols, transcendentals=0
        ),
    )(scal, bit, norm_gain[None], inputs[0], target[0], numerators[0], moment[0], second[0])
    return (outs[0][None], outs[1][None], outs[2][None], outs[3][0, :1])


def solution(mesh):
    shard = P("rep", "fsdp", None)
    return jax.shard_map(
        local,
        mesh=mesh,
        in_specs=(shard, shard, P(), shard, shard, shard, P("rep"), P()),
        out_specs=(shard, shard, shard, P("rep")),
        check_vma=False,
    )
```

```python
from functools import partial

import jax
import jax.numpy as jnp
from jax import lax
from jax.sharding import PartitionSpec as P

eps_norm = 1e-06
beta_one = 0.9
beta_two = 0.95
learn_rate = 0.001
decay_rate = 0.1
eps_adam = 1e-08
pieces = 4


def from_partner(block, axis, bit):
    count = lax.axis_size(axis)
    route = []
    for low in range(count):
        high = low | 1 << bit
        if high != low and high < count:
            route += [(low, high), (high, low)]
    return lax.ppermute(block, axis, route)


def local(inputs, target, norm_gain, numerators, moment, second, push_weight, step_index):
    values = inputs[0].astype(jnp.float32)
    inv_rms = lax.rsqrt(jnp.mean(values * values, axis=-1, keepdims=True) + eps_norm)
    normed = (values * inv_rms * norm_gain).astype(jnp.bfloat16)
    own_weight = push_weight[0]
    steps_done = step_index[0].astype(jnp.float32)
    fix_one = 1.0 - jnp.power(jnp.float32(beta_one), steps_done)
    fix_two = 1.0 - jnp.power(jnp.float32(beta_two), steps_done)
    bit_count = lax.axis_size("rep").bit_length() - 1
    bit_index = step_index[0] % bit_count
    current = numerators[0] / own_weight
    weight_low = current.astype(jnp.bfloat16)
    width = numerators.shape[2] // pieces

    def swap(block):
        theirs = from_partner(block, "rep", 0)
        for level in range(1, bit_count):
            theirs = jnp.where(bit_index == level, from_partner(block, "rep", level), theirs)
        return theirs

    whole = []
    for piece in range(pieces):
        rows = weight_low[:, piece * width : (piece + 1) * width]
        if whole:
            rows, whole[-1] = lax.optimization_barrier((rows, whole[-1]))
        whole.append(lax.all_gather(rows, "fsdp", axis=0, tiled=True))
    sums = []
    for piece in range(pieces):
        cut = slice(piece * width, (piece + 1) * width)
        projected = jnp.dot(normed, whole[piece], preferred_element_type=jnp.float32)
        key_error = (projected - target[0][:, cut].astype(jnp.float32)).astype(jnp.bfloat16)
        term = lax.dot_general(
            normed, key_error, (((0,), (0,)), ((), ())), preferred_element_type=jnp.float32
        )
        if sums:
            term, sums[-1] = lax.optimization_barrier((term, sums[-1]))
        sums.append(lax.psum_scatter(term, "fsdp", scatter_dimension=0, tiled=True))
    mixed, moments, seconds = [], [], []
    for piece in range(pieces):
        cut = slice(piece * width, (piece + 1) * width)
        gradient = sums[piece]
        new_moment = beta_one * moment[0][:, cut] + (1.0 - beta_one) * gradient
        new_second = beta_two * second[0][:, cut] + (1.0 - beta_two) * gradient * gradient
        direction = new_moment / fix_one / (jnp.sqrt(new_second / fix_two) + eps_adam)
        here = current[:, cut]
        updated = here - learn_rate * (direction + decay_rate * here)
        shares = own_weight * updated
        mixed.append((shares + swap(shares)) * 0.5)
        moments.append(new_moment)
        seconds.append(new_second)
    new_weight = (push_weight + swap(push_weight)) * 0.5
    join = partial(jnp.concatenate, axis=1)
    return (join(mixed)[None], join(moments)[None], join(seconds)[None], new_weight)


def solution(mesh):
    placed = (
        P("rep", "fsdp", None),
        P("rep", "fsdp", None),
        P(),
        P("rep", "fsdp", None),
        P("rep", "fsdp", None),
        P("rep", "fsdp", None),
        P("rep"),
        P(),
    )
    return jax.shard_map(
        local,
        mesh=mesh,
        in_specs=placed,
        out_specs=(
            P("rep", "fsdp", None),
            P("rep", "fsdp", None),
            P("rep", "fsdp", None),
            P("rep"),
        ),
        check_vma=False,
    )
```
